512 devices in a mesh: rows: 64 (over z, y), cols: 8 (over x, core).
Axes of the slice: x: 4, y: 8, z: 8, core: 2. Of those that a mesh axis runs over, the one named last changes fastest.
Arguments:
- archive: float32 [98304, 4096], P('rows', 'cols'), may hold values from -6 to 6
- sketch: float32 [4096, 512], P('cols'), may hold values from -0.09375 to 0.09375
Outputs:
- scaled_basis: float32 [98304, 512], P(('rows', 'cols'))
- projected: float32 [4096, 512], P(('cols', 'rows'))
The draws below stay inside these ranges and needn't reach their ends.
All inputs are finite; a program needn't handle non-finite values.
Results may differ from the reference program's by a relative error of at most 0.0003.
Values sent between devices are 32-bit elements; how exact they have to be, the bound alone decides.
No kernel may reach another device: no remote copies, remote signals or barrier semaphores. Data moves between devices by JAX's collectives and lax.ppermute only.
A program may use at most 64 MiB of HBM per device.

```python
import math
import jax
import jax.numpy as jnp
from jax import lax

N = 4096
K = 512
ROWS = 98304


def level_of(key, dims, cuts, low, largest):
    def one(axis_at, shards_of):
        steps = jax.random.uniform(jax.random.fold_in(jax.random.fold_in(key, 6), axis_at), (shards_of,), jnp.float32, low / len(cuts), largest / len(cuts))
        return jnp.repeat(jnp.exp(steps), dims[axis_at] // shards_of).reshape((-1,) + (1,) * (len(dims) - axis_at - 1))

    factor_of = one(*cuts[0])
    for cut in cuts[1:]:
        factor_of = factor_of * one(*cut)
    return factor_of


def bell_draw(rng, shape, width, reach, cuts=(), kind=jnp.bfloat16):
    result = width * jax.random.normal(rng, shape, jnp.float32)
    if cuts:
        result = result * level_of(rng, shape, cuts, -0.22, 0.18)
    return jnp.clip(result, -reach, reach).astype(kind)


def setup_inputs(seed: int = 0) -> dict:
    splits = jax.random.split(jax.random.key(seed), 3)
    archive = bell_draw(splits[0], (ROWS, N), 1.0, 6.0, ((0, 64), (1, 8)), jnp.float32)
    sketch = bell_draw(splits[1], (N, K), N ** -0.5, 0.09375, ((0, 8),), jnp.float32)
    return dict(archive=archive, sketch=sketch)


def reference(archive, sketch):
    precise = lax.Precision.HIGHEST
    images = jnp.dot(archive.astype(jnp.float32), sketch.astype(jnp.float32), precision=precise, preferred_element_type=jnp.float32)
    basis, upper = jnp.linalg.qr(images)
    signs = jnp.where(jnp.diagonal(upper) < 0, -1.0, 1.0).astype(basis.dtype)
    basis = basis * signs[None, :]
    projected = lax.dot_general(archive.astype(jnp.float32), basis.astype(jnp.float32), (((0,), (0,)), ((), ())), precision=precise, preferred_element_type=jnp.float32)
    return (basis * math.sqrt(ROWS), projected)
```

```python
import functools
import math

import jax
import jax.numpy as jnp
from jax import lax
from jax.experimental import pallas as pl
from jax.experimental.pallas import tpu as pltpu
from jax.sharding import Mesh
from jax.sharding import PartitionSpec as P

CORES = 2
BLOCK = 128
F32 = jnp.float32
BF16 = jnp.bfloat16
HIGHEST = lax.Precision.HIGHEST
VMEM = 48 * 2**20


def exact_dot(a, b, contract):
    return lax.dot_general(
        a, b, (contract, ((), ())), precision=HIGHEST, preferred_element_type=F32
    )


def halves(a):
    high = a.astype(BF16)
    return high, (a - high.astype(F32)).astype(BF16)


def three_pass_dot(a, b, contract):
    (a_high, a_low), (b_high, b_low) = a, b
    dot = functools.partial(
        lax.dot_general,
        dimension_numbers=(contract, ((), ())),
        preferred_element_type=F32,
    )
    return dot(a_high, b_high) + (dot(a_high, b_low) + dot(a_low, b_high))


def images_kernel(archive_ref, sketch_ref, out_ref, high_ref, low_ref):
    @pl.when(pl.program_id(0) == 0)
    def _():
        high_ref[...], low_ref[...] = halves(sketch_ref[...])

    out_ref[...] = three_pass_dot(
        halves(archive_ref[...]), (high_ref[...], low_ref[...]), ((1,), (0,))
    )


def partial_images(archive, sketch, groups):
    rows, depth = archive.shape
    width = sketch.shape[1]
    block = rows // (groups * CORES)
    return pl.pallas_call(
        images_kernel,
        grid=(groups * CORES,),
        in_specs=[
            pl.BlockSpec((block, depth), lambda i: (i % groups * CORES + i // groups, 0)),
            pl.BlockSpec((depth, width), lambda i: (0, 0)),
        ],
        out_specs=pl.BlockSpec((block, width), lambda i: (i, 0)),
        out_shape=jax.ShapeDtypeStruct((rows, width), F32),
        scratch_shapes=[pltpu.VMEM((depth, width), BF16)] * 2,
        compiler_params=pltpu.CompilerParams(vmem_limit_bytes=VMEM),
        cost_estimate=pl.CostEstimate(
            flops=6 * rows * depth * width, bytes_accessed=8 * rows * depth, transcendentals=0
        ),
    )(archive, sketch)


def products_kernel(slab_rows, place_ref, archive_ref, images_ref, gram_ref, moved_ref, slab_ref):
    step = pl.program_id(0)
    first = pl.multiple_of(place_ref[0] * BLOCK, BLOCK)

    @pl.when(step == 0)
    def _():
        moved_ref[...] = jnp.zeros_like(moved_ref)
        slab_ref[...] = jnp.zeros_like(slab_ref)

    images = halves(images_ref[...])
    moved_ref[...] += three_pass_dot(halves(archive_ref[...]), images, ((0,), (0,)))
    slab_ref[...] += three_pass_dot(halves(images_ref[:, pl.ds(first, BLOCK)]), images, ((0,), (0,)))

    @pl.when(step == pl.num_programs(0) - 1)
    def _():
        inside = pl.multiple_of(place_ref[1] * slab_rows, slab_rows)
        gram_ref[...] = slab_ref[pl.ds(inside, slab_rows), :]


def products(archive, images, position, groups, slab_rows):
    rows, depth = archive.shape
    width = images.shape[1]
    block = rows // (groups * CORES)
    slabs = BLOCK // slab_rows
    place = jnp.stack([position // slabs, position % slabs]).astype(jnp.int32)
    return pl.pallas_call(
        functools.partial(products_kernel, slab_rows),
        grid_spec=pltpu.PrefetchScalarGridSpec(
            num_scalar_prefetch=1,
            grid=(groups * CORES,),
            in_specs=[
                pl.BlockSpec((block, depth), lambda i, place: (i % groups * CORES + i // groups, 0)),
                pl.BlockSpec((block, width), lambda i, place: (i, 0)),
            ],
            out_specs=[
                pl.BlockSpec((slab_rows, width), lambda i, place: (0, 0)),
                pl.BlockSpec((depth, width), lambda i, place: (0, 0)),
            ],
            scratch_shapes=[pltpu.VMEM((BLOCK, width), F32)],
        ),
        out_shape=[
            jax.ShapeDtypeStruct((slab_rows, width), F32),
            jax.ShapeDtypeStruct((depth, width), F32),
        ],
        compiler_params=pltpu.CompilerParams(vmem_limit_bytes=VMEM),
        cost_estimate=pl.CostEstimate(
            flops=8 * rows * depth * width, bytes_accessed=8 * rows * depth, transcendentals=0
        ),
    )(place, archive, images)


def factor_block(rows):
    shape = rows[0].shape
    lane = lax.broadcasted_iota(jnp.int32, shape, 1)
    sub = lax.broadcasted_iota(jnp.int32, shape, 0)
    count = len(rows)
    result = []

    def column(slab, at):
        return jnp.broadcast_to(slab[:, at : at + 1], shape)

    def row(slab, at):
        return jnp.broadcast_to(slab[at : at + 1, :], shape)

    for p in range(count):
        panel = rows[p]
        columns = [column(panel, 8 * p + j) for j in range(8)]
        kept = jnp.zeros(shape, F32)
        roots = jnp.zeros(shape, F32)
        for j in range(8):
            here = lane == 8 * p + j
            at = sub == j
            pivot = row(columns[j], j)
            inverse = 1.0 / pivot
            current = jnp.where(here, 1.0, row(panel, j))
            kept = jnp.where(at, current, kept)
            roots = jnp.where(at, lax.rsqrt(pivot), roots)
            scaled = current * inverse
            panel = jnp.where(at, scaled, jnp.where(here, 0.0, panel) - columns[j] * scaled)
            for k in range(j + 1, 8):
                part = row(columns[k], j) * inverse
                columns[k] = jnp.where(at, part, columns[k] - columns[j] * part)
        result.append(jnp.where(lane <= sub + 8 * p, kept * roots, 0.0))
        own = (lane >= 8 * p) & (lane < 8 * p + 8)
        spread = [row(panel, j) for j in range(8)]
        for i in range(p + 1, count):
            terms = [column(rows[i], 8 * p + j) * spread[j] for j in range(8)]
            while len(terms) > 1:
                terms = [terms[a] + terms[a + 1] for a in range(0, len(terms), 2)]
            rows[i] = jnp.where(own, 0.0, rows[i]) - terms[0]
    return result


def factor_kernel(scale, gram_ref, images_ref, inverse_ref, basis_ref, work_ref, small_ref, panel_ref):
    size = gram_ref.shape[0]
    blocks = size // BLOCK
    work_ref[...] = gram_ref[...]
    column = lax.broadcasted_iota(jnp.int32, (BLOCK, size), 1)
    unit = (
        lax.broadcasted_iota(jnp.int32, (BLOCK, BLOCK), 0)
        == lax.broadcasted_iota(jnp.int32, (BLOCK, BLOCK), 1)
    ).astype(F32)

    def block_step(k, carry):
        first = pl.multiple_of(k * BLOCK, BLOCK)
        here = pl.ds(first, BLOCK)
        slabs = factor_block([work_ref[pl.ds(first + 8 * i, 8), here] for i in range(BLOCK // 8)])
        for i, slab in enumerate(slabs):
            small_ref[8 * i : 8 * i + 8, :] = slab
        work_ref[here, here] = unit
        panel = exact_dot(small_ref[...], work_ref[here, :], ((1,), (0,)))
        panel_ref[...] = panel
        finished = jnp.where(column < first + BLOCK, panel, 0.0)
        inverse_ref[here, :] = finished
        own = (column >= first) & (column < first + BLOCK)

        def update(i, inner):
            there = pl.ds(pl.multiple_of(i * BLOCK, BLOCK), BLOCK)
            kept = jnp.where(own, 0.0, work_ref[there, :])
            work_ref[there, :] = kept - exact_dot(panel_ref[:, there], panel_ref[...], ((0,), (0,)))
            return inner

        lax.fori_loop(k + 1, blocks, update, 0)
        basis_ref[:, here] = scale * exact_dot(images_ref[...], finished, ((1,), (1,)))
        return carry

    lax.fori_loop(0, blocks, block_step, 0)


def factor(gram, images, scale):
    size = gram.shape[0]
    return pl.pallas_call(
        functools.partial(factor_kernel, scale),
        in_specs=[pl.BlockSpec(memory_space=pltpu.VMEM)] * 2,
        out_specs=[pl.BlockSpec(memory_space=pltpu.VMEM)] * 2,
        out_shape=[
            jax.ShapeDtypeStruct(gram.shape, F32),
            jax.ShapeDtypeStruct(images.shape, F32),
        ],
        scratch_shapes=[
            pltpu.VMEM((size, size), F32),
            pltpu.VMEM((BLOCK, BLOCK), F32),
            pltpu.VMEM((BLOCK, size), F32),
        ],
        compiler_params=pltpu.CompilerParams(vmem_limit_bytes=VMEM),
        cost_estimate=pl.CostEstimate(
            flops=40 * size**3, bytes_accessed=12 * size**2, transcendentals=2 * size
        ),
    )(gram, images)


def exchange(blocks, axes):
    return lax.all_to_all(blocks, axes, 0, 0, tiled=True)


def gather(block, axes):
    size = lax.axis_size(axes)
    return exchange(jnp.broadcast_to(block[None], (size, *block.shape)), axes)


def local(archive, sketch):
    groups = lax.axis_size("x")
    over_rows = ("z", "y")
    stacked = lax.axis_size("z") * lax.axis_size("y")
    rows_here = archive.shape[0]
    width = sketch.shape[1]
    own_rows = rows_here // (groups * CORES)
    slab_rows = width // (groups * CORES)
    scale = math.sqrt(rows_here * stacked)

    partial = partial_images(archive, sketch, groups)
    by_core = exchange(partial.reshape(CORES, groups * own_rows, width), "core").sum(0)
    own_images = exchange(by_core.reshape(groups, own_rows, width), "x").sum(0)
    core_images = gather(own_images, "x").reshape(groups * own_rows, width)
    images = gather(core_images, "core").reshape(rows_here, width)

    position = lax.axis_index("core") * groups + lax.axis_index("x")
    gram, moved = products(archive, images, position, groups, slab_rows)

    moved = lax.psum_scatter(moved, "z", scatter_dimension=0, tiled=True)
    moved = lax.psum_scatter(moved, "y", scatter_dimension=0, tiled=True)

    pieces = gram.reshape(stacked, -1, BLOCK)
    gram = gather(exchange(pieces, over_rows).reshape(stacked, *pieces.shape[1:]).sum(0), over_rows)
    gram = gather(gather(gram.reshape(slab_rows, width), "x").reshape(groups * slab_rows, width), "core")
    inverse, basis = factor(gram.reshape(width, width), own_images, scale)
    return basis, exact_dot(moved, inverse, ((1,), (1,)))


def solution(mesh):
    rows, cols = mesh.devices.shape
    across = math.isqrt(rows)
    fine = Mesh(
        mesh.devices.reshape(rows // across, across, cols // CORES, CORES), ("z", "y", "x", "core")
    )
    return jax.shard_map(
        local,
        mesh=fine,
        in_specs=(P(("z", "y"), ("x", "core")), P(("x", "core"), None)),
        out_specs=(P(("z", "y", "x", "core"), None), P(("x", "core", "z", "y"), None)),
        check_vma=False,
    )
```

```python
import functools
import math

import jax
import jax.numpy as jnp
from jax import lax
from jax.experimental import pallas as pl
from jax.experimental.pallas import tpu as pltpu
from jax.sharding import Mesh
from jax.sharding import PartitionSpec as P

CORES = 2
BLOCK = 128
GROUP = 4
F32 = jnp.float32
BF16 = jnp.bfloat16
HIGHEST = lax.Precision.HIGHEST
VMEM = 48 * 2**20


def exact_dot(a, b, contract):
    return lax.dot_general(
        a, b, (contract, ((), ())), precision=HIGHEST, preferred_element_type=F32
    )


def halves(a):
    high = a.astype(BF16)
    return high, (a - high.astype(F32)).astype(BF16)


def three_pass_dot(a, b, axis_a, axis_b):
    left = jnp.concatenate([part for high, low in a for part in (high, low, high)], axis_a)
    right = jnp.concatenate([part for high, low in b for part in (high, high, low)], axis_b)
    return lax.dot_general(
        left, right, (((axis_a,), (axis_b,)), ((), ())), preferred_element_type=F32
    )


def thirds(a):
    high = a.astype(BF16)
    rest = a - high.astype(F32)
    middle = rest.astype(BF16)
    return high, middle, (rest - middle.astype(F32)).astype(BF16)


def six_pass_dot(a, b, axis_a, axis_b):
    a0, a1, a2 = thirds(a)
    b0, b1, b2 = thirds(b)
    left = jnp.concatenate([a0, a0, a1, a0, a2, a1], axis_a)
    right = jnp.concatenate([b0, b1, b0, b2, b0, b1], axis_b)
    return lax.dot_general(
        left, right, (((axis_a,), (axis_b,)), ((), ())), preferred_element_type=F32
    )


def row_block(place, device, flip):
    return device * CORES + (1 - place[0] if flip else place[0])


def images_kernel(place_ref, archive_ref, sketch_ref, out_ref, sketch_halves):
    depth = sketch_ref.shape[0]

    @pl.when(pl.program_id(0) == 0)
    def _():
        high, low = halves(sketch_ref[...])
        sketch_halves[:depth] = high
        sketch_halves[depth : 2 * depth] = high
        sketch_halves[2 * depth :] = low

    high, low = halves(archive_ref[...])
    out_ref[...] = jnp.dot(
        jnp.concatenate([high, low, high], 1), sketch_halves[...], preferred_element_type=F32
    )


def partial_images(archive, sketch, place, groups, flip):
    rows, depth = archive.shape
    width = sketch.shape[1]
    block = rows // (groups * CORES)
    return pl.pallas_call(
        images_kernel,
        grid_spec=pltpu.PrefetchScalarGridSpec(
            num_scalar_prefetch=1,
            grid=(groups,),
            in_specs=[
                pl.BlockSpec((block, depth), lambda i, place: (row_block(place, i, flip), 0)),
                pl.BlockSpec((depth, width), lambda i, place: (0, 0)),
            ],
            out_specs=pl.BlockSpec((block, width), lambda i, place: (i, 0)),
            scratch_shapes=[pltpu.VMEM((3 * depth, width), BF16)],
        ),
        out_shape=jax.ShapeDtypeStruct((groups * block, width), F32),
        compiler_params=pltpu.CompilerParams(vmem_limit_bytes=VMEM),
        cost_estimate=pl.CostEstimate(
            flops=3 * rows * depth * width, bytes_accessed=8 * rows * depth, transcendentals=0
        ),
    )(place, archive, sketch)


def whole(shape):
    return pl.BlockSpec(shape, lambda i, place: (0,) * len(shape))


def gram_kernel(place_ref, images_ref, kept_ref, sent_ref):
    rows = kept_ref.shape[0]
    images = halves(images_ref[...])
    for core, out_ref in ((place_ref[0], kept_ref), (1 - place_ref[0], sent_ref)):
        columns = pl.ds(pl.multiple_of(core * rows, rows), rows)
        out_ref[...] = three_pass_dot([halves(images_ref[:, columns])], [images], 0, 0)


def gram_halves(images, place):
    rows, width = images.shape
    shape = (width // CORES, width)
    return pl.pallas_call(
        gram_kernel,
        grid_spec=pltpu.PrefetchScalarGridSpec(
            num_scalar_prefetch=1,
            grid=(1,),
            in_specs=[whole(images.shape)],
            out_specs=[whole(shape)] * CORES,
        ),
        out_shape=[jax.ShapeDtypeStruct(shape, F32)] * CORES,
        compiler_params=pltpu.CompilerParams(vmem_limit_bytes=VMEM),
        cost_estimate=pl.CostEstimate(
            flops=6 * rows * width * width, bytes_accessed=4 * rows * width, transcendentals=0
        ),
    )(place, images)


def moved_kernel(count, place_ref, *refs):
    archive = [halves(ref[...]) for ref in refs[:count]]
    images = [halves(ref[...]) for ref in refs[count : 2 * count]]
    refs[-1][...] = three_pass_dot(archive, images, 0, 0)


def moved_rows(archive, near, far, place, groups):
    rows, depth = archive.shape
    block, width = near[0].shape

    def chosen(shift, flip):
        def at(i, place):
            return row_block(place, lax.rem(place[1] - shift + groups, groups), flip), 0

        return pl.BlockSpec((block, depth), at)

    images = [*near, *far]
    return pl.pallas_call(
        functools.partial(moved_kernel, len(images)),
        grid_spec=pltpu.PrefetchScalarGridSpec(
            num_scalar_prefetch=1,
            grid=(1,),
            in_specs=[chosen(shift, flip) for flip in (False, True) for shift in range(groups)]
            + [whole(part.shape) for part in images],
            out_specs=whole((depth, width)),
        ),
        out_shape=jax.ShapeDtypeStruct((depth, width), F32),
        compiler_params=pltpu.CompilerParams(vmem_limit_bytes=VMEM),
        cost_estimate=pl.CostEstimate(
            flops=6 * rows * depth * width, bytes_accessed=8 * rows * depth, transcendentals=0
        ),
    )(place, *([archive] * len(images)), *images)


def factor_block(rows):
    shape = rows[0].shape
    lane = lax.broadcasted_iota(jnp.int32, shape, 1)
    sub = lax.broadcasted_iota(jnp.int32, shape, 0)
    count = len(rows)
    result = []

    def column(slab, at):
        return jnp.broadcast_to(slab[:, at : at + 1], shape)

    def row(slab, at):
        return jnp.broadcast_to(slab[at : at + 1, :], shape)

    for group in range(0, count, GROUP):
        end = group + GROUP
        finished = []
        for p in range(group, end):
            panel = rows[p]
            columns = [column(panel, 8 * p + j) for j in range(8)]
            kept = jnp.zeros(shape, F32)
            pivots = jnp.zeros(shape, F32)
            for j in range(8):
                here = lane == 8 * p + j
                at = sub == j
                pivot = row(columns[j], j)
                inverse = 1.0 / pivot
                current = jnp.where(here, 1.0, row(panel, j))
                kept = jnp.where(at, current, kept)
                pivots = jnp.where(at, pivot, pivots)
                scaled = current * inverse
                panel = jnp.where(at, scaled, jnp.where(here, 0.0, panel) - columns[j] * scaled)
                for k in range(j + 1, 8):
                    part = row(columns[k], j) * inverse
                    columns[k] = jnp.where(at, part, columns[k] - columns[j] * part)
            finished.append(kept * lax.rsqrt(pivots))
            own = (lane >= 8 * p) & (lane < 8 * p + 8)
            spread = [row(panel, j) for j in range(8)]
            for i in range(p + 1, end):
                terms = [column(rows[i], 8 * p + j) * spread[j] for j in range(8)]
                while len(terms) > 1:
                    terms = [terms[a] + terms[a + 1] for a in range(0, len(terms), 2)]
                rows[i] = jnp.where(own, 0.0, rows[i]) - terms[0]
        lower = [lane <= sub + 8 * p for p in range(group, end)]
        result += [jnp.where(keep, slab, 0.0) for keep, slab in zip(lower, finished)]
        if end < count:
            later = lane >= 8 * end
            panel = jnp.concatenate(
                [jnp.where(keep | later, slab, 0.0) for keep, slab in zip(lower, finished)], 0
            )
            change = six_pass_dot(panel, panel, 0, 0)
            own = (lane >= 8 * group) & (lane < 8 * end)
            for i in range(end, count):
                rows[i] = jnp.where(own, 0.0, rows[i]) - change[8 * i : 8 * i + 8]
    return result


def factor_kernel(scale, groups, place_ref, images_ref, *refs):
    gram_refs = refs[: 2 * groups]
    inverse_ref, basis_ref, work_ref, small_ref, panel_ref = refs[2 * groups :]
    size = work_ref.shape[0]
    blocks = size // BLOCK
    slab = gram_refs[0].shape[0]
    for flip in range(CORES):
        core = 1 - place_ref[0] if flip else place_ref[0]
        for shift in range(groups):
            owner = lax.rem(place_ref[1] - shift + groups, groups)
            first = pl.multiple_of((core * groups + owner) * slab, slab)
            work_ref[pl.ds(first, slab), :] = gram_refs[flip * groups + shift][...]
    column = lax.broadcasted_iota(jnp.int32, (BLOCK, size), 1)
    unit = (
        lax.broadcasted_iota(jnp.int32, (BLOCK, BLOCK), 0)
        == lax.broadcasted_iota(jnp.int32, (BLOCK, BLOCK), 1)
    ).astype(F32)

    def block_step(k, carry):
        first = pl.multiple_of(k * BLOCK, BLOCK)
        here = pl.ds(first, BLOCK)
        slabs = factor_block([work_ref[pl.ds(first + 8 * i, 8), here] for i in range(BLOCK // 8)])
        for i, rows in enumerate(slabs):
            small_ref[8 * i : 8 * i + 8, :] = rows
        work_ref[here, here] = unit
        panel = six_pass_dot(small_ref[...], work_ref[here, :], 1, 0)
        panel_ref[...] = panel
        finished = jnp.where(column < first + BLOCK, panel, 0.0)
        inverse_ref[here, :] = finished
        own = (column >= first) & (column < first + BLOCK)

        def update(i, inner):
            there = pl.ds(pl.multiple_of(i * BLOCK, BLOCK), BLOCK)
            kept = jnp.where(own, 0.0, work_ref[there, :])
            work_ref[there, :] = kept - six_pass_dot(panel_ref[:, there], panel_ref[...], 0, 0)
            return inner

        lax.fori_loop(k + 1, blocks, update, 0)
        basis_ref[:, here] = scale * six_pass_dot(images_ref[...], finished, 1, 1)
        return carry

    lax.fori_loop(0, blocks, block_step, 0)


def factor(pieces, images, place, scale):
    size = images.shape[1]

    return pl.pallas_call(
        functools.partial(factor_kernel, scale, len(pieces) // CORES),
        grid_spec=pltpu.PrefetchScalarGridSpec(
            num_scalar_prefetch=1,
            grid=(1,),
            in_specs=[whole(part.shape) for part in (images, *pieces)],
            out_specs=[whole((size, size)), whole(images.shape)],
            scratch_shapes=[
                pltpu.VMEM((size, size), F32),
                pltpu.VMEM((BLOCK, BLOCK), F32),
                pltpu.VMEM((BLOCK, size), F32),
            ],
        ),
        out_shape=[
            jax.ShapeDtypeStruct((size, size), F32),
            jax.ShapeDtypeStruct(images.shape, F32),
        ],
        compiler_params=pltpu.CompilerParams(vmem_limit_bytes=VMEM),
        cost_estimate=pl.CostEstimate(
            flops=2 * size**2, bytes_accessed=size, transcendentals=2 * size
        ),
    )(place, images, *pieces)


def exchange(blocks, axes):
    return lax.all_to_all(blocks, axes, 0, 0, tiled=True)


def gather(block, axes):
    size = lax.axis_size(axes)
    return exchange(jnp.broadcast_to(block[None], (size, *block.shape)), axes)


def shifted(block, axis, by):
    size = lax.axis_size(axis)
    return lax.ppermute(block, axis, [(i, (i + by) % size) for i in range(size)])


def local(archive, sketch):
    groups = lax.axis_size("x")
    over_rows = ("z", "y")
    stacked = lax.axis_size("z") * lax.axis_size("y")
    rows_here = archive.shape[0]
    width = sketch.shape[1]
    own_rows = rows_here // (groups * CORES)
    slab_rows = width // (groups * CORES)
    scale = math.sqrt(rows_here * stacked)
    place = jnp.stack([lax.axis_index("core"), lax.axis_index("x")]).astype(jnp.int32)

    theirs = partial_images(archive, sketch, place, groups, True)
    mine = partial_images(archive, sketch, place, groups, False)
    sums = mine + shifted(theirs, "core", 1)
    own = exchange(sums.reshape(groups, own_rows, width), "x").sum(0)

    kept, sent = gram_halves(own, place)
    gram = kept + shifted(sent, "core", 1)
    gram = exchange(gram.reshape(groups, slab_rows, width), "x").sum(0)
    split = gram.reshape(stacked, -1, BLOCK)
    split, late = lax.optimization_barrier((split, own))
    row = exchange(split, over_rows).sum(0).reshape(split.shape[1:])

    near = [late, *(shifted(late, "x", s) for s in range(1, groups))]
    row, near = lax.optimization_barrier((row, near))
    far = shifted(jnp.concatenate(near, 0), "core", 1)
    far = [far[s * own_rows : (s + 1) * own_rows] for s in range(groups)]
    moved = moved_rows(archive, near, far, place, groups)

    gram = gather(row, over_rows).reshape(slab_rows, width)
    moved = exchange(moved.reshape(stacked, -1, width), over_rows)
    here = [gram, *(shifted(gram, "x", s) for s in range(1, groups))]
    there = shifted(jnp.concatenate(here, 0), "core", 1)
    there = [there[s * slab_rows : (s + 1) * slab_rows] for s in range(groups)]
    inverse, basis = factor(here + there, own, place, scale)
    return basis, exact_dot(moved.sum(0), inverse, ((1,), (1,)))


def solution(mesh):
    rows, cols = mesh.devices.shape
    across = math.isqrt(rows)
    fine = Mesh(
        mesh.devices.reshape(rows // across, across, cols // CORES, CORES), ("z", "y", "x", "core")
    )
    return jax.shard_map(
        local,
        mesh=fine,
        in_specs=(P(("z", "y"), ("x", "core")), P(("x", "core"), None)),
        out_specs=(P(("z", "y", "x", "core"), None), P(("x", "core", "z", "y"), None)),
        check_vma=False,
    )
```

```python
import functools
import math

import jax
import jax.numpy as jnp
from jax import lax
from jax.experimental import pallas as pl
from jax.experimental.pallas import tpu as pltpu
from jax.sharding import Mesh
from jax.sharding import PartitionSpec as P

CORES = 2
BLOCK = 128
GROUP = 2
AHEAD = 2
F32 = jnp.float32
BF16 = jnp.bfloat16
HIGHEST = lax.Precision.HIGHEST
VMEM = 48 * 2**20


def exact_dot(a, b, contract):
    return lax.dot_general(
        a, b, (contract, ((), ())), precision=HIGHEST, preferred_element_type=F32
    )


def halves(a):
    high = a.astype(BF16)
    return high, (a - high.astype(F32)).astype(BF16)


def three_pass_dot(a, b, axis_a, axis_b):
    left = jnp.concatenate([part for high, low in a for part in (high, low, high)], axis_a)
    right = jnp.concatenate([part for high, low in b for part in (high, high, low)], axis_b)
    return lax.dot_general(
        left, right, (((axis_a,), (axis_b,)), ((), ())), preferred_element_type=F32
    )


def thirds(a):
    high = a.astype(BF16)
    rest = a - high.astype(F32)
    middle = rest.astype(BF16)
    return high, middle, (rest - middle.astype(F32)).astype(BF16)


def six_pass_dot(a, b, axis_a, axis_b):
    a0, a1, a2 = thirds(a)
    b0, b1, b2 = thirds(b)
    left = jnp.concatenate([a0, a0, a1, a0, a2, a1], axis_a)
    right = jnp.concatenate([b0, b1, b0, b2, b0, b1], axis_b)
    return lax.dot_general(
        left, right, (((axis_a,), (axis_b,)), ((), ())), preferred_element_type=F32
    )


def row_block(place, device, flip):
    return device * CORES + (1 - place[0] if flip else place[0])


def images_kernel(place_ref, archive_ref, sketch_ref, out_ref, sketch_halves):
    depth = sketch_ref.shape[0]

    @pl.when(pl.program_id(0) == 0)
    def _():
        high, low = halves(sketch_ref[...])
        sketch_halves[:depth] = high
        sketch_halves[depth : 2 * depth] = high
        sketch_halves[2 * depth :] = low

    high, low = halves(archive_ref[...])
    out_ref[...] = jnp.dot(
        jnp.concatenate([high, low, high], 1), sketch_halves[...], preferred_element_type=F32
    )


def partial_images(archive, sketch, place, groups, flip):
    rows, depth = archive.shape
    width = sketch.shape[1]
    block = rows // (groups * CORES)
    return pl.pallas_call(
        images_kernel,
        grid_spec=pltpu.PrefetchScalarGridSpec(
            num_scalar_prefetch=1,
            grid=(groups,),
            in_specs=[
                pl.BlockSpec((block, depth), lambda i, place: (row_block(place, i, flip), 0)),
                pl.BlockSpec((depth, width), lambda i, place: (0, 0)),
            ],
            out_specs=pl.BlockSpec((block, width), lambda i, place: (i, 0)),
            scratch_shapes=[pltpu.VMEM((3 * depth, width), BF16)],
        ),
        out_shape=jax.ShapeDtypeStruct((groups * block, width), F32),
        compiler_params=pltpu.CompilerParams(vmem_limit_bytes=VMEM),
        cost_estimate=pl.CostEstimate(
            flops=3 * rows * depth * width, bytes_accessed=8 * rows * depth, transcendentals=0
        ),
    )(place, archive, sketch)


def whole(shape):
    return pl.BlockSpec(shape, lambda i, place: (0,) * len(shape))


def upper_blocks(size):
    count = size // BLOCK
    return [(i, j) for i in range(count) for j in range(i, count)]


def gram_kernel(place_ref, images_ref, kept_ref, sent_ref):
    high, low = halves(images_ref[...])
    left = jnp.concatenate([high, low, high], 0)
    right = jnp.concatenate([high, high, low], 0)
    size = left.shape[1]
    blocks = []
    for first in range(0, size, BLOCK):
        panel = lax.dot_general(
            left[:, first : first + BLOCK],
            right[:, first:],
            (((0,), (0,)), ((), ())),
            preferred_element_type=F32,
        )
        blocks += [panel[:, at : at + BLOCK] for at in range(0, size - first, BLOCK)]
    per = len(blocks) // CORES
    is_first = place_ref[0] == 0
    for n in range(per):
        rows = pl.ds(n * BLOCK, BLOCK)
        kept_ref[rows, :] = jnp.where(is_first, blocks[n], blocks[per + n])
        sent_ref[rows, :] = jnp.where(is_first, blocks[per + n], blocks[n])


def gram_halves(images, place):
    rows, width = images.shape
    shape = (len(upper_blocks(width)) // CORES * BLOCK, BLOCK)
    return pl.pallas_call(
        gram_kernel,
        grid_spec=pltpu.PrefetchScalarGridSpec(
            num_scalar_prefetch=1,
            grid=(1,),
            in_specs=[whole(images.shape)],
            out_specs=[whole(shape)] * CORES,
        ),
        out_shape=[jax.ShapeDtypeStruct(shape, F32)] * CORES,
        compiler_params=pltpu.CompilerParams(vmem_limit_bytes=VMEM),
        cost_estimate=pl.CostEstimate(
            flops=6 * rows * width * width, bytes_accessed=4 * rows * width, transcendentals=0
        ),
    )(place, images)


def moved_kernel(count, place_ref, *refs):
    archive = [halves(ref[...]) for ref in refs[:count]]
    images = [halves(ref[...]) for ref in refs[count : 2 * count]]
    refs[-1][...] = three_pass_dot(archive, images, 0, 0)


def moved_rows(archive, near, far, place, groups):
    rows, depth = archive.shape
    block, width = near[0].shape

    def chosen(shift, flip):
        def at(i, place):
            return row_block(place, lax.rem(place[1] - shift + groups, groups), flip), 0

        return pl.BlockSpec((block, depth), at)

    images = [*near, *far]
    return pl.pallas_call(
        functools.partial(moved_kernel, len(images)),
        grid_spec=pltpu.PrefetchScalarGridSpec(
            num_scalar_prefetch=1,
            grid=(1,),
            in_specs=[chosen(shift, flip) for flip in (False, True) for shift in range(groups)]
            + [whole(part.shape) for part in images],
            out_specs=whole((depth, width)),
        ),
        out_shape=jax.ShapeDtypeStruct((depth, width), F32),
        compiler_params=pltpu.CompilerParams(vmem_limit_bytes=VMEM),
        cost_estimate=pl.CostEstimate(
            flops=6 * rows * depth * width, bytes_accessed=8 * rows * depth, transcendentals=0
        ),
    )(place, *([archive] * len(images)), *images)


def factor_block(rows):
    shape = rows[0].shape
    lane = lax.broadcasted_iota(jnp.int32, shape, 1)
    sub = lax.broadcasted_iota(jnp.int32, shape, 0)
    count = len(rows)
    result = []

    def column(slab, at):
        return jnp.broadcast_to(slab[:, at : at + 1], shape)

    def row(slab, at):
        return jnp.broadcast_to(slab[at : at + 1, :], shape)

    for group in range(0, count, GROUP):
        end = group + GROUP
        reach = min(end + AHEAD, count)
        finished = []
        for p in range(group, end):
            panel, base = rows[p], 8 * p
            own = (lane >= base) & (lane < base + 8)
            columns = [column(panel, base + j) for j in range(8)]
            small = [[row(columns[k], i) for k in range(i + 1)] for i in range(8)]
            across = [
                jnp.where(lane == base + j, 1.0, jnp.where(own, 0.0, row(panel, j))) for j in range(8)
            ]
            later = range(p + 1, reach)
            down = {i: [column(rows[i], base + j) for j in range(8)] for i in later}
            for i in later:
                rows[i] = jnp.where(own, 0.0, rows[i])
            kept = jnp.zeros(shape, F32)
            pivots = jnp.zeros(shape, F32)
            for j in range(8):
                inverse = 1.0 / small[j][j]
                ratio = {i: small[i][j] * inverse for i in range(j + 1, 8)}
                for i in range(j + 1, 8):
                    for k in range(j + 1, i + 1):
                        small[i][k] = small[i][k] - ratio[i] * small[k][j]
                    across[i] = across[i] - ratio[i] * across[j]
                scaled = across[j] * inverse
                for i in later:
                    for k in range(j + 1, 8):
                        down[i][k] = down[i][k] - down[i][j] * ratio[k]
                    rows[i] = rows[i] - down[i][j] * scaled
                kept = jnp.where(sub == j, across[j], kept)
                pivots = jnp.where(sub == j, small[j][j], pivots)
            finished.append(kept * lax.rsqrt(pivots))
        lower = [lane <= sub + 8 * p for p in range(group, end)]
        result += [jnp.where(keep, slab, 0.0) for keep, slab in zip(lower, finished)]
        if reach < count:
            right = lane >= 8 * end
            panel = jnp.concatenate(
                [jnp.where(keep | right, slab, 0.0) for keep, slab in zip(lower, finished)], 0
            )
            change = six_pass_dot(panel, panel, 0, 0)
            own = (lane >= 8 * group) & (lane < 8 * end)
            for i in range(reach, count):
                rows[i] = jnp.where(own, 0.0, rows[i]) - change[8 * i : 8 * i + 8]
    return result


def factor_kernel(scale, groups, place_ref, images_ref, *refs):
    gram_refs = refs[: 2 * groups]
    inverse_ref, basis_ref, packed_ref, work_ref = refs[2 * groups :]
    size = work_ref.shape[0]
    slab = gram_refs[0].shape[0]
    for flip in range(CORES):
        core = 1 - place_ref[0] if flip else place_ref[0]
        for shift in range(groups):
            owner = lax.rem(place_ref[1] - shift + groups, groups)
            first = pl.multiple_of((core * groups + owner) * slab, slab)
            packed_ref[pl.ds(first, slab), :] = gram_refs[flip * groups + shift][...]
    work_ref[...] = jnp.zeros_like(work_ref)
    for n, (i, j) in enumerate(upper_blocks(size)):
        work_ref[i * BLOCK : (i + 1) * BLOCK, j * BLOCK : (j + 1) * BLOCK] = packed_ref[
            n * BLOCK : (n + 1) * BLOCK, :
        ]
    unit = (
        lax.broadcasted_iota(jnp.int32, (BLOCK, BLOCK), 0)
        == lax.broadcasted_iota(jnp.int32, (BLOCK, BLOCK), 1)
    ).astype(F32)

    diagonal = packed_ref[:BLOCK, :]
    for first in range(0, size, BLOCK):
        end = first + BLOCK
        slabs = factor_block([diagonal[8 * i : 8 * i + 8] for i in range(BLOCK // 8)])
        work_ref[first:end, first:end] = unit
        panel = six_pass_dot(jnp.concatenate(slabs, 0), work_ref[first:end, :], 1, 0)
        finished = panel[:, :end]
        if end < size:
            following = panel[:, end : end + BLOCK]
            diagonal = work_ref[end : end + BLOCK, end : end + BLOCK]
            diagonal = diagonal - six_pass_dot(following, following, 0, 0)
            change = six_pass_dot(panel[:, end:], panel, 0, 0)
            if first:
                work_ref[end:, :first] = work_ref[end:, :first] - change[:, :first]
            work_ref[end:, first:end] = -change[:, first:end]
            work_ref[end:, end:] = work_ref[end:, end:] - change[:, end:]
            inverse_ref[first:end, end:] = jnp.zeros((BLOCK, size - end), F32)
        inverse_ref[first:end, :end] = finished
        basis_ref[:, first:end] = scale * six_pass_dot(images_ref[:, :end], finished, 1, 1)


def factor(pieces, images, place, scale):
    size = images.shape[1]

    return pl.pallas_call(
        functools.partial(factor_kernel, scale, len(pieces) // CORES),
        grid_spec=pltpu.PrefetchScalarGridSpec(
            num_scalar_prefetch=1,
            grid=(1,),
            in_specs=[whole(part.shape) for part in (images, *pieces)],
            out_specs=[whole((size, size)), whole(images.shape)],
            scratch_shapes=[
                pltpu.VMEM((len(upper_blocks(size)) * BLOCK, BLOCK), F32),
                pltpu.VMEM((size, size), F32),
            ],
        ),
        out_shape=[
            jax.ShapeDtypeStruct((size, size), F32),
            jax.ShapeDtypeStruct(images.shape, F32),
        ],
        compiler_params=pltpu.CompilerParams(vmem_limit_bytes=VMEM),
        cost_estimate=pl.CostEstimate(
            flops=2 * size**2, bytes_accessed=size, transcendentals=2 * size
        ),
    )(place, images, *pieces)


def exchange(blocks, axes):
    return lax.all_to_all(blocks, axes, 0, 0, tiled=True)


def gather(block, axes):
    size = lax.axis_size(axes)
    return exchange(jnp.broadcast_to(block[None], (size, *block.shape)), axes)


def shifted(block, axis, by):
    size = lax.axis_size(axis)
    return lax.ppermute(block, axis, [(i, (i + by) % size) for i in range(size)])


def local(archive, sketch):
    groups = lax.axis_size("x")
    over_rows = ("z", "y")
    stacked = lax.axis_size("z") * lax.axis_size("y")
    rows_here = archive.shape[0]
    width = sketch.shape[1]
    own_rows = rows_here // (groups * CORES)
    slab_rows = len(upper_blocks(width)) * BLOCK // (groups * CORES)
    scale = math.sqrt(rows_here * stacked)
    place = jnp.stack([lax.axis_index("core"), lax.axis_index("x")]).astype(jnp.int32)

    theirs = partial_images(archive, sketch, place, groups, True)
    mine = partial_images(archive, sketch, place, groups, False)
    sums = mine + shifted(theirs, "core", 1)
    own = exchange(sums.reshape(groups, own_rows, width), "x").sum(0)

    kept, sent = gram_halves(own, place)
    gram = kept + shifted(sent, "core", 1)
    gram = exchange(gram.reshape(groups, slab_rows, BLOCK), "x").sum(0)
    per = pl.cdiv(slab_rows, stacked)
    split = jnp.pad(gram, ((0, per * stacked - slab_rows), (0, 0))).reshape(stacked, per, BLOCK)
    row = exchange(split, over_rows).sum(0)

    near = [own, *(shifted(own, "x", s) for s in range(1, groups))]
    row, near = lax.optimization_barrier((row, near))
    far = shifted(jnp.concatenate(near, 0), "core", 1)
    far = [far[s * own_rows : (s + 1) * own_rows] for s in range(groups)]
    moved = moved_rows(archive, near, far, place, groups)

    gram = gather(row, over_rows).reshape(per * stacked, BLOCK)[:slab_rows]
    moved = exchange(moved.reshape(stacked, -1, width), over_rows)
    here = [gram, *(shifted(gram, "x", s) for s in range(1, groups))]
    there = shifted(jnp.concatenate(here, 0), "core", 1)
    there = [there[s * slab_rows : (s + 1) * slab_rows] for s in range(groups)]
    inverse, basis = factor(here + there, own, place, scale)
    return basis, exact_dot(moved.sum(0), inverse, ((1,), (1,)))


def solution(mesh):
    rows, cols = mesh.devices.shape
    across = math.isqrt(rows)
    fine = Mesh(
        mesh.devices.reshape(rows // across, across, cols // CORES, CORES), ("z", "y", "x", "core")
    )
    return jax.shard_map(
        local,
        mesh=fine,
        in_specs=(P(("z", "y"), ("x", "core")), P(("x", "core"), None)),
        out_specs=(P(("z", "y", "x", "core"), None), P(("x", "core", "z", "y"), None)),
        check_vma=False,
    )
```

```python
import functools
import math

import jax
import jax.numpy as jnp
from jax import lax
from jax.experimental import pallas as pl
from jax.experimental.pallas import tpu as pltpu
from jax.sharding import Mesh
from jax.sharding import PartitionSpec as P

CORES = 2
BLOCK = 128
GROUP = 2
AHEAD = 2
F32 = jnp.float32
BF16 = jnp.bfloat16
HIGHEST = lax.Precision.HIGHEST
VMEM = 48 * 2**20


def exact_dot(a, b, contract):
    return lax.dot_general(
        a, b, (contract, ((), ())), precision=HIGHEST, preferred_element_type=F32
    )


def halves(a):
    high = a.astype(BF16)
    return high, (a - high.astype(F32)).astype(BF16)


def three_pass_dot(a, b, axis_a, axis_b):
    left = jnp.concatenate([part for high, low in a for part in (high, low, high)], axis_a)
    right = jnp.concatenate([part for high, low in b for part in (high, high, low)], axis_b)
    return lax.dot_general(
        left, right, (((axis_a,), (axis_b,)), ((), ())), preferred_element_type=F32
    )


def thirds(a):
    high = a.astype(BF16)
    rest = a - high.astype(F32)
    middle = rest.astype(BF16)
    return high, middle, (rest - middle.astype(F32)).astype(BF16)


def six_pass_dot(a, b, axis_a, axis_b):
    a0, a1, a2 = thirds(a)
    b0, b1, b2 = thirds(b)
    left = jnp.concatenate([a0, a0, a1, a0, a2, a1], axis_a)
    right = jnp.concatenate([b0, b1, b0, b2, b0, b1], axis_b)
    return lax.dot_general(
        left, right, (((axis_a,), (axis_b,)), ((), ())), preferred_element_type=F32
    )


def row_block(place, device, flip):
    return device * CORES + (1 - place[0] if flip else place[0])


def images_kernel(place_ref, archive_ref, sketch_ref, out_ref, sketch_halves):
    depth = sketch_ref.shape[0]

    @pl.when(pl.program_id(0) == 0)
    def _():
        high, low = halves(sketch_ref[...])
        sketch_halves[:depth] = high
        sketch_halves[depth : 2 * depth] = high
        sketch_halves[2 * depth :] = low

    high, low = halves(archive_ref[...])
    out_ref[...] = jnp.dot(
        jnp.concatenate([high, low, high], 1), sketch_halves[...], preferred_element_type=F32
    )


def partial_images(archive, sketch, place, groups, flip):
    rows, depth = archive.shape
    width = sketch.shape[1]
    block = rows // (groups * CORES)
    return pl.pallas_call(
        images_kernel,
        grid_spec=pltpu.PrefetchScalarGridSpec(
            num_scalar_prefetch=1,
            grid=(groups,),
            in_specs=[
                pl.BlockSpec((block, depth), lambda i, place: (row_block(place, i, flip), 0)),
                pl.BlockSpec((depth, width), lambda i, place: (0, 0)),
            ],
            out_specs=pl.BlockSpec((block, width), lambda i, place: (i, 0)),
            scratch_shapes=[pltpu.VMEM((3 * depth, width), BF16)],
        ),
        out_shape=jax.ShapeDtypeStruct((groups * block, width), F32),
        compiler_params=pltpu.CompilerParams(vmem_limit_bytes=VMEM),
        cost_estimate=pl.CostEstimate(
            flops=3 * rows * depth * width, bytes_accessed=8 * rows * depth, transcendentals=0
        ),
    )(place, archive, sketch)


def whole(shape):
    return pl.BlockSpec(shape, lambda i, place: (0,) * len(shape))


def upper_blocks(size):
    count = size // BLOCK
    return [(i, j) for i in range(count) for j in range(i, count)]


def gram_kernel(place_ref, images_ref, kept_ref, sent_ref):
    high, low = halves(images_ref[...])
    left = jnp.concatenate([high, low, high], 0)
    right = jnp.concatenate([high, high, low], 0)
    size = left.shape[1]
    blocks = []
    for first in range(0, size, BLOCK):
        panel = lax.dot_general(
            left[:, first : first + BLOCK],
            right[:, first:],
            (((0,), (0,)), ((), ())),
            preferred_element_type=F32,
        )
        blocks += [panel[:, at : at + BLOCK] for at in range(0, size - first, BLOCK)]
    per = len(blocks) // CORES
    is_first = place_ref[0] == 0
    for n in range(per):
        rows = pl.ds(n * BLOCK, BLOCK)
        kept_ref[rows, :] = jnp.where(is_first, blocks[n], blocks[per + n])
        sent_ref[rows, :] = jnp.where(is_first, blocks[per + n], blocks[n])


def gram_halves(images, place):
    rows, width = images.shape
    shape = (len(upper_blocks(width)) // CORES * BLOCK, BLOCK)
    return pl.pallas_call(
        gram_kernel,
        grid_spec=pltpu.PrefetchScalarGridSpec(
            num_scalar_prefetch=1,
            grid=(1,),
            in_specs=[whole(images.shape)],
            out_specs=[whole(shape)] * CORES,
        ),
        out_shape=[jax.ShapeDtypeStruct(shape, F32)] * CORES,
        compiler_params=pltpu.CompilerParams(vmem_limit_bytes=VMEM),
        cost_estimate=pl.CostEstimate(
            flops=6 * rows * width * width, bytes_accessed=4 * rows * width, transcendentals=0
        ),
    )(place, images)


def moved_kernel(count, place_ref, *refs):
    archive = [halves(ref[...]) for ref in refs[:count]]
    images = [halves(ref[...]) for ref in refs[count : 2 * count]]
    refs[-1][...] = three_pass_dot(archive, images, 0, 0)


def moved_rows(archive, near, far, place, groups):
    rows, depth = archive.shape
    block, width = near[0].shape

    def chosen(shift, flip):
        def at(i, place):
            return row_block(place, lax.rem(place[1] - shift + groups, groups), flip), 0

        return pl.BlockSpec((block, depth), at)

    images = [*near, *far]
    return pl.pallas_call(
        functools.partial(moved_kernel, len(images)),
        grid_spec=pltpu.PrefetchScalarGridSpec(
            num_scalar_prefetch=1,
            grid=(1,),
            in_specs=[chosen(shift, flip) for flip in (False, True) for shift in range(groups)]
            + [whole(part.shape) for part in images],
            out_specs=whole((depth, width)),
        ),
        out_shape=jax.ShapeDtypeStruct((depth, width), F32),
        compiler_params=pltpu.CompilerParams(vmem_limit_bytes=VMEM),
        cost_estimate=pl.CostEstimate(
            flops=6 * rows * depth * width, bytes_accessed=8 * rows * depth, transcendentals=0
        ),
    )(place, *([archive] * len(images)), *images)


def factor_block(rows, spread_ref):
    shape = rows[0].shape
    lane = lax.broadcasted_iota(jnp.int32, shape, 1)
    sub = lax.broadcasted_iota(jnp.int32, shape, 0)
    count = len(rows)
    result = []

    def column(slab, at):
        return jnp.broadcast_to(slab[:, at : at + 1], shape)

    def row(slab, at):
        return jnp.broadcast_to(slab[at : at + 1, :], shape)

    for group in range(0, count, GROUP):
        end = group + GROUP
        reach = min(end + AHEAD, count)
        finished = []
        for p in range(group, end):
            panel, base = rows[p], 8 * p
            own = (lane >= base) & (lane < base + 8)
            columns = [column(panel, base + j) for j in range(8)]
            side = p % 2
            for k, slab in enumerate([*columns, jnp.where(own, (lane == base + sub).astype(F32), panel)]):
                spread_ref[side, 8 * k : 8 * k + 8, :] = slab

            def spread(k, i):
                return jnp.broadcast_to(spread_ref[side, 8 * k + i : 8 * k + i + 1, :], shape)

            small = [[spread(k, i) for k in range(i + 1)] for i in range(8)]
            across = [spread(8, j) for j in range(8)]
            later = range(p + 1, reach)
            down = {i: [column(rows[i], base + j) for j in range(8)] for i in later}
            for i in later:
                rows[i] = jnp.where(own, 0.0, rows[i])
            kept = jnp.zeros(shape, F32)
            pivots = jnp.zeros(shape, F32)
            sizes = [1.0 / small[j][j] for j in range(0, 8, 2)]
            for j in range(0, 8, 2):
                n, rest = j + 1, range(j + 2, 8)
                size = sizes[j // 2]
                a, b, c = small[j][j] * size, small[n][j] * size, small[n][n]
                determinant = a * c - b * small[n][j]
                inverse = 1.0 / determinant
                first = {i: (c * (small[i][j] * size) - b * small[i][n]) * inverse for i in rest}
                second = {i: (a * small[i][n] - b * small[i][j]) * inverse for i in rest}
                for i in rest:
                    for k in range(j + 2, i + 1):
                        change = first[i] * small[k][j] + second[i] * small[k][n]
                        small[i][k] = small[i][k] - change
                for i in rest:
                    across[i] = across[i] - (first[i] * across[j] + second[i] * across[n])
                mixed = b * inverse
                upper = (c * inverse) * size * across[j] - mixed * across[n]
                under = (a * inverse) * across[n] - mixed * across[j]
                for i in later:
                    for k in rest:
                        change = down[i][j] * first[k] + down[i][n] * second[k]
                        down[i][k] = down[i][k] - change
                    rows[i] = rows[i] - (down[i][j] * upper + down[i][n] * under)
                reciprocal = 1.0 / a
                kept = jnp.where(sub == j, across[j], kept)
                kept = jnp.where(sub == n, across[n] - (b * reciprocal) * across[j], kept)
                pivots = jnp.where(sub == j, small[j][j], pivots)
                pivots = jnp.where(sub == n, determinant * reciprocal, pivots)
            finished.append(kept * lax.rsqrt(pivots))
        lower = [lane <= sub + 8 * p for p in range(group, end)]
        result += [jnp.where(keep, slab, 0.0) for keep, slab in zip(lower, finished)]
        if reach < count:
            right = lane >= 8 * end
            panel = jnp.concatenate(
                [jnp.where(keep | right, slab, 0.0) for keep, slab in zip(lower, finished)], 0
            )
            change = six_pass_dot(panel, panel, 0, 0)
            own = (lane >= 8 * group) & (lane < 8 * end)
            for i in range(reach, count):
                rows[i] = jnp.where(own, 0.0, rows[i]) - change[8 * i : 8 * i + 8]
    return result


def factor_kernel(scale, groups, place_ref, images_ref, *refs):
    gram_refs = refs[: 2 * groups]
    inverse_ref, basis_ref, packed_ref, work_ref, spread_ref = refs[2 * groups :]
    size = work_ref.shape[0]
    slab = gram_refs[0].shape[0]
    for flip in range(CORES):
        core = 1 - place_ref[0] if flip else place_ref[0]
        for shift in range(groups):
            owner = lax.rem(place_ref[1] - shift + groups, groups)
            first = pl.multiple_of((core * groups + owner) * slab, slab)
            packed_ref[pl.ds(first, slab), :] = gram_refs[flip * groups + shift][...]
    work_ref[...] = jnp.zeros_like(work_ref)
    for n, (i, j) in enumerate(upper_blocks(size)):
        work_ref[i * BLOCK : (i + 1) * BLOCK, j * BLOCK : (j + 1) * BLOCK] = packed_ref[
            n * BLOCK : (n + 1) * BLOCK, :
        ]
    unit = (
        lax.broadcasted_iota(jnp.int32, (BLOCK, BLOCK), 0)
        == lax.broadcasted_iota(jnp.int32, (BLOCK, BLOCK), 1)
    ).astype(F32)

    diagonal = packed_ref[:BLOCK, :]
    for first in range(0, size, BLOCK):
        end = first + BLOCK
        slabs = factor_block([diagonal[8 * i : 8 * i + 8] for i in range(BLOCK // 8)], spread_ref)
        work_ref[first:end, first:end] = unit
        panel = six_pass_dot(jnp.concatenate(slabs, 0), work_ref[first:end, :], 1, 0)
        finished = panel[:, :end]
        if end < size:
            following = panel[:, end : end + BLOCK]
            diagonal = work_ref[end : end + BLOCK, end : end + BLOCK]
            diagonal = diagonal - six_pass_dot(following, following, 0, 0)
            change = six_pass_dot(panel[:, end:], panel, 0, 0)
            if first:
                work_ref[end:, :first] = work_ref[end:, :first] - change[:, :first]
            work_ref[end:, first:end] = -change[:, first:end]
            work_ref[end:, end:] = work_ref[end:, end:] - change[:, end:]
            inverse_ref[first:end, end:] = jnp.zeros((BLOCK, size - end), F32)
        inverse_ref[first:end, :end] = finished
        basis_ref[:, first:end] = scale * six_pass_dot(images_ref[:, :end], finished, 1, 1)


def factor(pieces, images, place, scale):
    size = images.shape[1]

    return pl.pallas_call(
        functools.partial(factor_kernel, scale, len(pieces) // CORES),
        grid_spec=pltpu.PrefetchScalarGridSpec(
            num_scalar_prefetch=1,
            grid=(1,),
            in_specs=[whole(part.shape) for part in (images, *pieces)],
            out_specs=[whole((size, size)), whole(images.shape)],
            scratch_shapes=[
                pltpu.VMEM((len(upper_blocks(size)) * BLOCK, BLOCK), F32),
                pltpu.VMEM((size, size), F32),
                pltpu.VMEM((2, 72, BLOCK), F32),
            ],
        ),
        out_shape=[
            jax.ShapeDtypeStruct((size, size), F32),
            jax.ShapeDtypeStruct(images.shape, F32),
        ],
        compiler_params=pltpu.CompilerParams(vmem_limit_bytes=VMEM),
        cost_estimate=pl.CostEstimate(
            flops=2 * size**2, bytes_accessed=size, transcendentals=2 * size
        ),
    )(place, images, *pieces)


def exchange(blocks, axes):
    return lax.all_to_all(blocks, axes, 0, 0, tiled=True)


def gather(block, axes):
    size = lax.axis_size(axes)
    return exchange(jnp.broadcast_to(block[None], (size, *block.shape)), axes)


def shifted(block, axis, by):
    size = lax.axis_size(axis)
    return lax.ppermute(block, axis, [(i, (i + by) % size) for i in range(size)])


def local(archive, sketch):
    groups = lax.axis_size("x")
    over_rows = ("z", "y")
    stacked = lax.axis_size("z") * lax.axis_size("y")
    rows_here = archive.shape[0]
    width = sketch.shape[1]
    own_rows = rows_here // (groups * CORES)
    slab_rows = len(upper_blocks(width)) * BLOCK // (groups * CORES)
    scale = math.sqrt(rows_here * stacked)
    place = jnp.stack([lax.axis_index("core"), lax.axis_index("x")]).astype(jnp.int32)

    theirs = partial_images(archive, sketch, place, groups, True)
    mine = partial_images(archive, sketch, place, groups, False)
    sums = mine + shifted(theirs, "core", 1)
    own = exchange(sums.reshape(groups, own_rows, width), "x").sum(0)

    kept, sent = gram_halves(own, place)
    gram = kept + shifted(sent, "core", 1)
    gram = exchange(gram.reshape(groups, slab_rows, BLOCK), "x").sum(0)
    per = pl.cdiv(slab_rows, stacked)
    split = jnp.pad(gram, ((0, per * stacked - slab_rows), (0, 0))).reshape(stacked, per, BLOCK)
    row = exchange(split, over_rows).sum(0)

    near = [own, *(shifted(own, "x", s) for s in range(1, groups))]
    row, near = lax.optimization_barrier((row, near))
    far = shifted(jnp.concatenate(near, 0), "core", 1)
    far = [far[s * own_rows : (s + 1) * own_rows] for s in range(groups)]
    moved = moved_rows(archive, near, far, place, groups)

    gram = gather(row, over_rows).reshape(per * stacked, BLOCK)[:slab_rows]
    moved = exchange(moved.reshape(stacked, -1, width), over_rows)
    here = [gram, *(shifted(gram, "x", s) for s in range(1, groups))]
    there = shifted(jnp.concatenate(here, 0), "core", 1)
    there = [there[s * slab_rows : (s + 1) * slab_rows] for s in range(groups)]
    inverse, basis = factor(here + there, own, place, scale)
    return basis, exact_dot(moved.sum(0), inverse, ((1,), (1,)))


def solution(mesh):
    rows, cols = mesh.devices.shape
    across = math.isqrt(rows)
    fine = Mesh(
        mesh.devices.reshape(rows // across, across, cols // CORES, CORES), ("z", "y", "x", "core")
    )
    return jax.shard_map(
        local,
        mesh=fine,
        in_specs=(P(("z", "y"), ("x", "core")), P(("x", "core"), None)),
        out_specs=(P(("z", "y", "x", "core"), None), P(("x", "core", "z", "y"), None)),
        check_vma=False,
    )
```

```python
import functools
import math

import jax
import jax.numpy as jnp
from jax import lax
from jax.experimental import pallas as pl
from jax.experimental.pallas import tpu as pltpu
from jax.sharding import Mesh
from jax.sharding import PartitionSpec as P

CORES = 2
BLOCK = 128
GROUP = 2
AHEAD = 2
F32 = jnp.float32
BF16 = jnp.bfloat16
HIGHEST = lax.Precision.HIGHEST
VMEM = 48 * 2**20


def exact_dot(a, b, contract):
    return lax.dot_general(
        a, b, (contract, ((), ())), precision=HIGHEST, preferred_element_type=F32
    )


def halves(a):
    high = a.astype(BF16)
    return high, (a - high.astype(F32)).astype(BF16)


def three_pass_dot(a, b, axis_a, axis_b):
    left = jnp.concatenate([part for high, low in a for part in (high, low, high)], axis_a)
    right = jnp.concatenate([part for high, low in b for part in (high, high, low)], axis_b)
    return lax.dot_general(
        left, right, (((axis_a,), (axis_b,)), ((), ())), preferred_element_type=F32
    )


def thirds(a):
    high = a.astype(BF16)
    rest = a - high.astype(F32)
    middle = rest.astype(BF16)
    return high, middle, (rest - middle.astype(F32)).astype(BF16)


def six_pass_dot(a, b, axis_a, axis_b):
    a0, a1, a2 = thirds(a)
    b0, b1, b2 = thirds(b)
    left = jnp.concatenate([a0, a0, a1, a0, a2, a1], axis_a)
    right = jnp.concatenate([b0, b1, b0, b2, b0, b1], axis_b)
    return lax.dot_general(
        left, right, (((axis_a,), (axis_b,)), ((), ())), preferred_element_type=F32
    )


def row_block(place, device, flip):
    return device * CORES + (1 - place[0] if flip else place[0])


def images_kernel(place_ref, first_ref, second_ref, sketch_ref, out_ref, sketch_halves):
    depth = sketch_ref.shape[0]

    @pl.when(pl.program_id(0) == 0)
    def _():
        high, low = halves(sketch_ref[...])
        sketch_halves[:depth] = high
        sketch_halves[depth : 2 * depth] = high
        sketch_halves[2 * depth :] = low

    high, low = halves(jnp.concatenate([first_ref[...], second_ref[...]], 0))
    out_ref[...] = jnp.dot(
        jnp.concatenate([high, low, high], 1), sketch_halves[...], preferred_element_type=F32
    )


def partial_images(archive, sketch, place, groups, flip):
    rows, depth = archive.shape
    width = sketch.shape[1]
    block = rows // (groups * CORES)
    return pl.pallas_call(
        images_kernel,
        grid_spec=pltpu.PrefetchScalarGridSpec(
            num_scalar_prefetch=1,
            grid=(groups // 2,),
            in_specs=[
                pl.BlockSpec((block, depth), lambda i, place: (row_block(place, 2 * i, flip), 0)),
                pl.BlockSpec((block, depth), lambda i, place: (row_block(place, 2 * i + 1, flip), 0)),
                pl.BlockSpec((depth, width), lambda i, place: (0, 0)),
            ],
            out_specs=pl.BlockSpec((2 * block, width), lambda i, place: (i, 0)),
            scratch_shapes=[pltpu.VMEM((3 * depth, width), BF16)],
        ),
        out_shape=jax.ShapeDtypeStruct((groups * block, width), F32),
        compiler_params=pltpu.CompilerParams(vmem_limit_bytes=VMEM),
        cost_estimate=pl.CostEstimate(
            flops=3 * rows * depth * width, bytes_accessed=8 * rows * depth, transcendentals=0
        ),
    )(place, archive, archive, sketch)


def whole(shape):
    return pl.BlockSpec(shape, lambda i, place: (0,) * len(shape))


def upper_blocks(size):
    count = size // BLOCK
    return [(i, j) for i in range(count) for j in range(i, count)]


def gram_kernel(place_ref, images_ref, kept_ref, sent_ref):
    high, low = halves(images_ref[...])
    left = jnp.concatenate([high, low, high], 0)
    right = jnp.concatenate([high, high, low], 0)
    size = left.shape[1]
    blocks = []
    for first in range(0, size, BLOCK):
        panel = lax.dot_general(
            left[:, first : first + BLOCK],
            right[:, first:],
            (((0,), (0,)), ((), ())),
            preferred_element_type=F32,
        )
        blocks += [panel[:, at : at + BLOCK] for at in range(0, size - first, BLOCK)]
    per = len(blocks) // CORES
    is_first = place_ref[0] == 0
    for n in range(per):
        rows = pl.ds(n * BLOCK, BLOCK)
        kept_ref[rows, :] = jnp.where(is_first, blocks[n], blocks[per + n])
        sent_ref[rows, :] = jnp.where(is_first, blocks[per + n], blocks[n])


def gram_halves(images, place):
    rows, width = images.shape
    shape = (len(upper_blocks(width)) // CORES * BLOCK, BLOCK)
    return pl.pallas_call(
        gram_kernel,
        grid_spec=pltpu.PrefetchScalarGridSpec(
            num_scalar_prefetch=1,
            grid=(1,),
            in_specs=[whole(images.shape)],
            out_specs=[whole(shape)] * CORES,
        ),
        out_shape=[jax.ShapeDtypeStruct(shape, F32)] * CORES,
        compiler_params=pltpu.CompilerParams(vmem_limit_bytes=VMEM),
        cost_estimate=pl.CostEstimate(
            flops=6 * rows * width * width, bytes_accessed=4 * rows * width, transcendentals=0
        ),
    )(place, images)


def moved_kernel(count, place_ref, *refs):
    archive = [halves(ref[...]) for ref in refs[:count]]
    images = [halves(ref[...]) for ref in refs[count : 2 * count]]
    refs[-1][...] = three_pass_dot(archive, images, 0, 0)


def moved_rows(archive, near, far, place, groups):
    rows, depth = archive.shape
    block, width = near[0].shape

    def chosen(shift, flip):
        def at(i, place):
            return row_block(place, lax.rem(place[1] - shift + groups, groups), flip), 0

        return pl.BlockSpec((block, depth), at)

    images = [*near, *far]
    return pl.pallas_call(
        functools.partial(moved_kernel, len(images)),
        grid_spec=pltpu.PrefetchScalarGridSpec(
            num_scalar_prefetch=1,
            grid=(1,),
            in_specs=[chosen(shift, flip) for flip in (False, True) for shift in range(groups)]
            + [whole(part.shape) for part in images],
            out_specs=whole((depth, width)),
        ),
        out_shape=jax.ShapeDtypeStruct((depth, width), F32),
        compiler_params=pltpu.CompilerParams(vmem_limit_bytes=VMEM),
        cost_estimate=pl.CostEstimate(
            flops=6 * rows * depth * width, bytes_accessed=8 * rows * depth, transcendentals=0
        ),
    )(place, *([archive] * len(images)), *images)


def factor_block(rows, spread_ref):
    shape = rows[0].shape
    lane = lax.broadcasted_iota(jnp.int32, shape, 1)
    sub = lax.broadcasted_iota(jnp.int32, shape, 0)
    count = len(rows)
    result = []

    def column(slab, at):
        return jnp.broadcast_to(slab[:, at : at + 1], shape)

    def row(slab, at):
        return jnp.broadcast_to(slab[at : at + 1, :], shape)

    for group in range(0, count, GROUP):
        end = group + GROUP
        reach = min(end + AHEAD, count)
        finished = []
        for p in range(group, end):
            panel, base = rows[p], 8 * p
            own = (lane >= base) & (lane < base + 8)
            columns = [column(panel, base + j) for j in range(8)]
            side = p % 2
            for k, slab in enumerate([*columns, jnp.where(own, (lane == base + sub).astype(F32), panel)]):
                spread_ref[side, 8 * k : 8 * k + 8, :] = slab

            def spread(k, i):
                return jnp.broadcast_to(spread_ref[side, 8 * k + i : 8 * k + i + 1, :], shape)

            small = [[spread(k, i) for k in range(i + 1)] for i in range(8)]
            across = [spread(8, j) for j in range(8)]
            later = range(p + 1, reach)
            down = {i: [column(rows[i], base + j) for j in range(8)] for i in later}
            for i in later:
                rows[i] = jnp.where(own, 0.0, rows[i])
            kept = jnp.zeros(shape, F32)
            pivots = jnp.zeros(shape, F32)
            sizes = [1.0 / small[j][j] for j in range(0, 8, 2)]
            for j in range(0, 8, 2):
                n, rest = j + 1, range(j + 2, 8)
                size = sizes[j // 2]
                a, b, c = small[j][j] * size, small[n][j] * size, small[n][n]
                determinant = a * c - b * small[n][j]
                inverse = 1.0 / determinant
                first = {i: (c * (small[i][j] * size) - b * small[i][n]) * inverse for i in rest}
                second = {i: (a * small[i][n] - b * small[i][j]) * inverse for i in rest}
                for i in rest:
                    for k in range(j + 2, i + 1):
                        change = first[i] * small[k][j] + second[i] * small[k][n]
                        small[i][k] = small[i][k] - change
                for i in rest:
                    across[i] = across[i] - (first[i] * across[j] + second[i] * across[n])
                mixed = b * inverse
                upper = (c * inverse) * size * across[j] - mixed * across[n]
                under = (a * inverse) * across[n] - mixed * across[j]
                for i in later:
                    for k in rest:
                        change = down[i][j] * first[k] + down[i][n] * second[k]
                        down[i][k] = down[i][k] - change
                    rows[i] = rows[i] - (down[i][j] * upper + down[i][n] * under)
                reciprocal = 1.0 / a
                kept = jnp.where(sub == j, across[j], kept)
                kept = jnp.where(sub == n, across[n] - (b * reciprocal) * across[j], kept)
                pivots = jnp.where(sub == j, small[j][j], pivots)
                pivots = jnp.where(sub == n, determinant * reciprocal, pivots)
            finished.append(kept * lax.rsqrt(pivots))
        lower = [lane <= sub + 8 * p for p in range(group, end)]
        result += [jnp.where(keep, slab, 0.0) for keep, slab in zip(lower, finished)]
        if reach < count:
            right = lane >= 8 * end
            panel = jnp.concatenate(
                [jnp.where(keep | right, slab, 0.0) for keep, slab in zip(lower, finished)], 0
            )
            change = six_pass_dot(panel, panel, 0, 0)
            own = (lane >= 8 * group) & (lane < 8 * end)
            for i in range(reach, count):
                rows[i] = jnp.where(own, 0.0, rows[i]) - change[8 * i : 8 * i + 8]
    return result


def factor_kernel(scale, groups, place_ref, images_ref, *refs):
    gram_refs = refs[: 2 * groups]
    inverse_ref, basis_ref, packed_ref, work_ref, spread_ref = refs[2 * groups :]
    size = work_ref.shape[0]
    slab = gram_refs[0].shape[0]
    for flip in range(CORES):
        core = 1 - place_ref[0] if flip else place_ref[0]
        for shift in range(groups):
            owner = lax.rem(place_ref[1] - shift + groups, groups)
            first = pl.multiple_of((core * groups + owner) * slab, slab)
            packed_ref[pl.ds(first, slab), :] = gram_refs[flip * groups + shift][...]
    work_ref[...] = jnp.zeros_like(work_ref)
    for n, (i, j) in enumerate(upper_blocks(size)):
        work_ref[i * BLOCK : (i + 1) * BLOCK, j * BLOCK : (j + 1) * BLOCK] = packed_ref[
            n * BLOCK : (n + 1) * BLOCK, :
        ]
    unit = (
        lax.broadcasted_iota(jnp.int32, (BLOCK, BLOCK), 0)
        == lax.broadcasted_iota(jnp.int32, (BLOCK, BLOCK), 1)
    ).astype(F32)

    diagonal = packed_ref[:BLOCK, :]
    for first in range(0, size, BLOCK):
        end = first + BLOCK
        slabs = factor_block([diagonal[8 * i : 8 * i + 8] for i in range(BLOCK // 8)], spread_ref)
        work_ref[first:end, first:end] = unit
        panel = six_pass_dot(jnp.concatenate(slabs, 0), work_ref[first:end, :], 1, 0)
        finished = panel[:, :end]
        if end < size:
            following = panel[:, end : end + BLOCK]
            diagonal = work_ref[end : end + BLOCK, end : end + BLOCK]
            diagonal = diagonal - six_pass_dot(following, following, 0, 0)
            change = six_pass_dot(panel[:, end:], panel, 0, 0)
            if first:
                work_ref[end:, :first] = work_ref[end:, :first] - change[:, :first]
            work_ref[end:, first:end] = -change[:, first:end]
            work_ref[end:, end:] = work_ref[end:, end:] - change[:, end:]
            inverse_ref[first:end, end:] = jnp.zeros((BLOCK, size - end), F32)
        inverse_ref[first:end, :end] = finished
        basis_ref[:, first:end] = scale * six_pass_dot(images_ref[:, :end], finished, 1, 1)


def factor(pieces, images, place, scale):
    size = images.shape[1]

    return pl.pallas_call(
        functools.partial(factor_kernel, scale, len(pieces) // CORES),
        grid_spec=pltpu.PrefetchScalarGridSpec(
            num_scalar_prefetch=1,
            grid=(1,),
            in_specs=[whole(part.shape) for part in (images, *pieces)],
            out_specs=[whole((size, size)), whole(images.shape)],
            scratch_shapes=[
                pltpu.VMEM((len(upper_blocks(size)) * BLOCK, BLOCK), F32),
                pltpu.VMEM((size, size), F32),
                pltpu.VMEM((2, 72, BLOCK), F32),
            ],
        ),
        out_shape=[
            jax.ShapeDtypeStruct((size, size), F32),
            jax.ShapeDtypeStruct(images.shape, F32),
        ],
        compiler_params=pltpu.CompilerParams(vmem_limit_bytes=VMEM),
        cost_estimate=pl.CostEstimate(
            flops=2 * size**2, bytes_accessed=size, transcendentals=2 * size
        ),
    )(place, images, *pieces)


def exchange(blocks, axes):
    return lax.all_to_all(blocks, axes, 0, 0, tiled=True)


def gather(block, axes):
    size = lax.axis_size(axes)
    return exchange(jnp.broadcast_to(block[None], (size, *block.shape)), axes)


def shifted(block, axis, by):
    size = lax.axis_size(axis)
    return lax.ppermute(block, axis, [(i, (i + by) % size) for i in range(size)])


def local(archive, sketch):
    groups = lax.axis_size("x")
    over_rows = ("z", "y")
    stacked = lax.axis_size("z") * lax.axis_size("y")
    rows_here = archive.shape[0]
    width = sketch.shape[1]
    own_rows = rows_here // (groups * CORES)
    slab_rows = len(upper_blocks(width)) * BLOCK // (groups * CORES)
    scale = math.sqrt(rows_here * stacked)
    place = jnp.stack([lax.axis_index("core"), lax.axis_index("x")]).astype(jnp.int32)

    theirs = partial_images(archive, sketch, place, groups, True)
    mine = partial_images(archive, sketch, place, groups, False)
    sums = mine + shifted(theirs, "core", 1)
    own = exchange(sums.reshape(groups, own_rows, width), "x").sum(0)

    kept, sent = gram_halves(own, place)
    gram = kept + shifted(sent, "core", 1)
    gram = exchange(gram.reshape(groups, slab_rows, BLOCK), "x").sum(0)
    across = lax.axis_size("y")
    per = pl.cdiv(slab_rows, across * 8) * 8
    split = jnp.pad(gram, ((0, per * across - slab_rows), (0, 0))).reshape(across, per, BLOCK)
    row = exchange(split, "y").sum(0)
    row = gather(row, "z").sum(0)

    near = [own, *(shifted(own, "x", s) for s in range(1, groups))]
    row, near = lax.optimization_barrier((row, near))
    far = shifted(jnp.concatenate(near, 0), "core", 1)
    far = [far[s * own_rows : (s + 1) * own_rows] for s in range(groups)]
    moved = moved_rows(archive, near, far, place, groups)

    gram = gather(row, "y").reshape(per * across, BLOCK)[:slab_rows]
    moved = exchange(moved.reshape(stacked, -1, width), over_rows)
    here = [gram, *(shifted(gram, "x", s) for s in range(1, groups))]
    there = shifted(jnp.concatenate(here, 0), "core", 1)
    there = [there[s * slab_rows : (s + 1) * slab_rows] for s in range(groups)]
    inverse, basis = factor(here + there, own, place, scale)
    return basis, exact_dot(moved.sum(0), inverse, ((1,), (1,)))


def solution(mesh):
    rows, cols = mesh.devices.shape
    across = math.isqrt(rows)
    fine = Mesh(
        mesh.devices.reshape(rows // across, across, cols // CORES, CORES), ("z", "y", "x", "core")
    )
    return jax.shard_map(
        local,
        mesh=fine,
        in_specs=(P(("z", "y"), ("x", "core")), P(("x", "core"), None)),
        out_specs=(P(("z", "y", "x", "core"), None), P(("x", "core", "z", "y"), None)),
        check_vma=False,
    )
```

```python
import functools
import math

import jax
import jax.numpy as jnp
from jax import lax
from jax.experimental import pallas as pl
from jax.experimental.pallas import tpu as pltpu
from jax.sharding import Mesh
from jax.sharding import PartitionSpec as P

CORES = 2
BLOCK = 128
GROUP = 2
AHEAD = 2
F32 = jnp.float32
BF16 = jnp.bfloat16
VMEM = 48 * 2**20


def last_dot(a, b, contract):
    return lax.dot_general(
        a, b, (contract, ((), ())), precision=lax.Precision.HIGH, preferred_element_type=F32
    )


def halves(a):
    high = a.astype(BF16)
    return high, (a - high.astype(F32)).astype(BF16)


def three_pass_dot(a, b, axis_a, axis_b):
    left = jnp.concatenate([part for high, low in a for part in (high, low, high)], axis_a)
    right = jnp.concatenate([part for high, low in b for part in (high, high, low)], axis_b)
    return lax.dot_general(
        left, right, (((axis_a,), (axis_b,)), ((), ())), preferred_element_type=F32
    )


def thirds(a):
    high = a.astype(BF16)
    rest = a - high.astype(F32)
    middle = rest.astype(BF16)
    return high, middle, (rest - middle.astype(F32)).astype(BF16)


def six_pass_dot(a, b, axis_a, axis_b):
    a0, a1, a2 = thirds(a)
    b0, b1, b2 = thirds(b)
    left = jnp.concatenate([a0, a0, a1, a0, a2, a1], axis_a)
    right = jnp.concatenate([b0, b1, b0, b2, b0, b1], axis_b)
    return lax.dot_general(
        left, right, (((axis_a,), (axis_b,)), ((), ())), preferred_element_type=F32
    )


def row_block(place, device, flip):
    return device * CORES + (1 - place[0] if flip else place[0])


def images_kernel(place_ref, first_ref, second_ref, sketch_ref, out_ref, sketch_halves):
    depth = sketch_ref.shape[0]

    @pl.when(pl.program_id(0) == 0)
    def _():
        high, low = halves(sketch_ref[...])
        sketch_halves[:depth] = high
        sketch_halves[depth : 2 * depth] = high
        sketch_halves[2 * depth :] = low

    high, low = halves(jnp.concatenate([first_ref[...], second_ref[...]], 0))
    out_ref[...] = jnp.dot(
        jnp.concatenate([high, low, high], 1), sketch_halves[...], preferred_element_type=F32
    )


def partial_images(archive, sketch, place, groups, flip):
    rows, depth = archive.shape
    width = sketch.shape[1]
    block = rows // (groups * CORES)
    return pl.pallas_call(
        images_kernel,
        grid_spec=pltpu.PrefetchScalarGridSpec(
            num_scalar_prefetch=1,
            grid=(groups // 2,),
            in_specs=[
                pl.BlockSpec((block, depth), lambda i, place: (row_block(place, 2 * i, flip), 0)),
                pl.BlockSpec((block, depth), lambda i, place: (row_block(place, 2 * i + 1, flip), 0)),
                pl.BlockSpec((depth, width), lambda i, place: (0, 0)),
            ],
            out_specs=pl.BlockSpec((2 * block, width), lambda i, place: (i, 0)),
            scratch_shapes=[pltpu.VMEM((3 * depth, width), BF16)],
        ),
        out_shape=jax.ShapeDtypeStruct((groups * block, width), F32),
        compiler_params=pltpu.CompilerParams(vmem_limit_bytes=VMEM),
        cost_estimate=pl.CostEstimate(
            flops=3 * rows * depth * width, bytes_accessed=8 * rows * depth, transcendentals=0
        ),
    )(place, archive, archive, sketch)


def whole(shape):
    return pl.BlockSpec(shape, lambda i, place: (0,) * len(shape))


def upper_blocks(size):
    count = size // BLOCK
    return [(i, j) for i in range(count) for j in range(i, count)]


def gram_kernel(place_ref, images_ref, kept_ref, sent_ref):
    high, low = halves(images_ref[...])
    left = jnp.concatenate([high, low, high], 0)
    right = jnp.concatenate([high, high, low], 0)
    size = left.shape[1]
    blocks = []
    for first in range(0, size, BLOCK):
        panel = lax.dot_general(
            left[:, first : first + BLOCK],
            right[:, first:],
            (((0,), (0,)), ((), ())),
            preferred_element_type=F32,
        )
        blocks += [panel[:, at : at + BLOCK] for at in range(0, size - first, BLOCK)]
    per = len(blocks) // CORES
    is_first = place_ref[0] == 0
    for n in range(per):
        rows = pl.ds(n * BLOCK, BLOCK)
        kept_ref[rows, :] = jnp.where(is_first, blocks[n], blocks[per + n])
        sent_ref[rows, :] = jnp.where(is_first, blocks[per + n], blocks[n])


def gram_halves(images, place):
    rows, width = images.shape
    shape = (len(upper_blocks(width)) // CORES * BLOCK, BLOCK)
    return pl.pallas_call(
        gram_kernel,
        grid_spec=pltpu.PrefetchScalarGridSpec(
            num_scalar_prefetch=1,
            grid=(1,),
            in_specs=[whole(images.shape)],
            out_specs=[whole(shape)] * CORES,
        ),
        out_shape=[jax.ShapeDtypeStruct(shape, F32)] * CORES,
        compiler_params=pltpu.CompilerParams(vmem_limit_bytes=VMEM),
        cost_estimate=pl.CostEstimate(
            flops=6 * rows * width * width, bytes_accessed=4 * rows * width, transcendentals=0
        ),
    )(place, images)


def moved_kernel(count, place_ref, *refs):
    archive = [halves(ref[...]) for ref in refs[:count]]
    images = [halves(ref[...]) for ref in refs[count : 2 * count]]
    refs[-1][...] = three_pass_dot(archive, images, 0, 0)


def moved_rows(archive, near, far, place, groups):
    rows, depth = archive.shape
    block, width = near[0].shape

    def chosen(shift, flip):
        def at(i, place):
            return row_block(place, lax.rem(place[1] - shift + groups, groups), flip), 0

        return pl.BlockSpec((block, depth), at)

    images = [*near, *far]
    return pl.pallas_call(
        functools.partial(moved_kernel, len(images)),
        grid_spec=pltpu.PrefetchScalarGridSpec(
            num_scalar_prefetch=1,
            grid=(1,),
            in_specs=[chosen(shift, flip) for flip in (False, True) for shift in range(groups)]
            + [whole(part.shape) for part in images],
            out_specs=whole((depth, width)),
        ),
        out_shape=jax.ShapeDtypeStruct((depth, width), F32),
        compiler_params=pltpu.CompilerParams(vmem_limit_bytes=VMEM),
        cost_estimate=pl.CostEstimate(
            flops=6 * rows * depth * width, bytes_accessed=8 * rows * depth, transcendentals=0
        ),
    )(place, *([archive] * len(images)), *images)


def factor_block(rows, spread_ref):
    shape = rows[0].shape
    lane = lax.broadcasted_iota(jnp.int32, shape, 1)
    sub = lax.broadcasted_iota(jnp.int32, shape, 0)
    count = len(rows)
    result = []

    def column(slab, at):
        return jnp.broadcast_to(slab[:, at : at + 1], shape)

    def row(slab, at):
        return jnp.broadcast_to(slab[at : at + 1, :], shape)

    for group in range(0, count, GROUP):
        end = group + GROUP
        reach = min(end + AHEAD, count)
        finished = []
        for p in range(group, end):
            panel, base = rows[p], 8 * p
            own = (lane >= base) & (lane < base + 8)
            columns = [column(panel, base + j) for j in range(8)]
            side = p % 2
            for k, slab in enumerate([*columns, jnp.where(own, (lane == base + sub).astype(F32), panel)]):
                spread_ref[side, 8 * k : 8 * k + 8, :] = slab

            def spread(k, i):
                return jnp.broadcast_to(spread_ref[side, 8 * k + i : 8 * k + i + 1, :], shape)

            small = [[spread(k, i) for k in range(i + 1)] for i in range(8)]
            across = [spread(8, j) for j in range(8)]
            later = range(p + 1, reach)
            down = {i: [column(rows[i], base + j) for j in range(8)] for i in later}
            for i in later:
                rows[i] = jnp.where(own, 0.0, rows[i])
            kept = jnp.zeros(shape, F32)
            pivots = jnp.zeros(shape, F32)
            sizes = [1.0 / small[j][j] for j in range(0, 8, 2)]
            for j in range(0, 8, 2):
                n, rest = j + 1, range(j + 2, 8)
                size = sizes[j // 2]
                a, b, c = small[j][j] * size, small[n][j] * size, small[n][n]
                determinant = a * c - b * small[n][j]
                inverse = 1.0 / determinant
                first = {i: (c * (small[i][j] * size) - b * small[i][n]) * inverse for i in rest}
                second = {i: (a * small[i][n] - b * small[i][j]) * inverse for i in rest}
                for i in rest:
                    for k in range(j + 2, i + 1):
                        change = first[i] * small[k][j] + second[i] * small[k][n]
                        small[i][k] = small[i][k] - change
                for i in rest:
                    across[i] = across[i] - (first[i] * across[j] + second[i] * across[n])
                mixed = b * inverse
                upper = (c * inverse) * size * across[j] - mixed * across[n]
                under = (a * inverse) * across[n] - mixed * across[j]
                for i in later:
                    for k in rest:
                        change = down[i][j] * first[k] + down[i][n] * second[k]
                        down[i][k] = down[i][k] - change
                    rows[i] = rows[i] - (down[i][j] * upper + down[i][n] * under)
                reciprocal = 1.0 / a
                kept = jnp.where(sub == j, across[j], kept)
                kept = jnp.where(sub == n, across[n] - (b * reciprocal) * across[j], kept)
                pivots = jnp.where(sub == j, small[j][j], pivots)
                pivots = jnp.where(sub == n, determinant * reciprocal, pivots)
            finished.append(kept * lax.rsqrt(pivots))
        lower = [lane <= sub + 8 * p for p in range(group, end)]
        result += [jnp.where(keep, slab, 0.0) for keep, slab in zip(lower, finished)]
        if reach < count:
            right = lane >= 8 * end
            panel = jnp.concatenate(
                [jnp.where(keep | right, slab, 0.0) for keep, slab in zip(lower, finished)], 0
            )
            change = six_pass_dot(panel, panel, 0, 0)
            own = (lane >= 8 * group) & (lane < 8 * end)
            for i in range(reach, count):
                rows[i] = jnp.where(own, 0.0, rows[i]) - change[8 * i : 8 * i + 8]
    return result


def factor_kernel(scale, groups, place_ref, images_ref, *refs):
    gram_refs = refs[: 2 * groups]
    inverse_ref, basis_ref, packed_ref, work_ref, spread_ref = refs[2 * groups :]
    size = work_ref.shape[0]
    slab = gram_refs[0].shape[0]
    for flip in range(CORES):
        core = 1 - place_ref[0] if flip else place_ref[0]
        for shift in range(groups):
            owner = lax.rem(place_ref[1] - shift + groups, groups)
            first = pl.multiple_of((core * groups + owner) * slab, slab)
            packed_ref[pl.ds(first, slab), :] = gram_refs[flip * groups + shift][...]
    work_ref[...] = jnp.zeros_like(work_ref)
    for n, (i, j) in enumerate(upper_blocks(size)):
        work_ref[i * BLOCK : (i + 1) * BLOCK, j * BLOCK : (j + 1) * BLOCK] = packed_ref[
            n * BLOCK : (n + 1) * BLOCK, :
        ]
    unit = (
        lax.broadcasted_iota(jnp.int32, (BLOCK, BLOCK), 0)
        == lax.broadcasted_iota(jnp.int32, (BLOCK, BLOCK), 1)
    ).astype(F32)

    diagonal = packed_ref[:BLOCK, :]
    for first in range(0, size, BLOCK):
        end = first + BLOCK
        slabs = factor_block([diagonal[8 * i : 8 * i + 8] for i in range(BLOCK // 8)], spread_ref)
        work_ref[first:end, first:end] = unit
        panel = six_pass_dot(jnp.concatenate(slabs, 0), work_ref[first:end, :], 1, 0)
        finished = panel[:, :end]
        if end < size:
            following = panel[:, end : end + BLOCK]
            diagonal = work_ref[end : end + BLOCK, end : end + BLOCK]
            diagonal = diagonal - six_pass_dot(following, following, 0, 0)
            change = six_pass_dot(panel[:, end:], panel, 0, 0)
            if first:
                work_ref[end:, :first] = work_ref[end:, :first] - change[:, :first]
            work_ref[end:, first:end] = -change[:, first:end]
            work_ref[end:, end:] = work_ref[end:, end:] - change[:, end:]
            inverse_ref[first:end, end:] = jnp.zeros((BLOCK, size - end), F32)
        inverse_ref[first:end, :end] = finished
        basis_ref[:, first:end] = scale * three_pass_dot(
            [halves(images_ref[:, :end])], [halves(finished)], 1, 1
        )


def factor(pieces, images, place, scale):
    size = images.shape[1]

    return pl.pallas_call(
        functools.partial(factor_kernel, scale, len(pieces) // CORES),
        grid_spec=pltpu.PrefetchScalarGridSpec(
            num_scalar_prefetch=1,
            grid=(1,),
            in_specs=[whole(part.shape) for part in (images, *pieces)],
            out_specs=[whole((size, size)), whole(images.shape)],
            scratch_shapes=[
                pltpu.VMEM((len(upper_blocks(size)) * BLOCK, BLOCK), F32),
                pltpu.VMEM((size, size), F32),
                pltpu.VMEM((2, 72, BLOCK), F32),
            ],
        ),
        out_shape=[
            jax.ShapeDtypeStruct((size, size), F32),
            jax.ShapeDtypeStruct(images.shape, F32),
        ],
        compiler_params=pltpu.CompilerParams(vmem_limit_bytes=VMEM),
        cost_estimate=pl.CostEstimate(
            flops=2 * size**2, bytes_accessed=size, transcendentals=2 * size
        ),
    )(place, images, *pieces)


def exchange(blocks, axes):
    return lax.all_to_all(blocks, axes, 0, 0, tiled=True)


def gather(block, axes):
    size = lax.axis_size(axes)
    return exchange(jnp.broadcast_to(block[None], (size, *block.shape)), axes)


def shifted(block, axis, by):
    size = lax.axis_size(axis)
    return lax.ppermute(block, axis, [(i, (i + by) % size) for i in range(size)])


def local(archive, sketch):
    groups = lax.axis_size("x")
    over_rows = ("z", "y")
    stacked = lax.axis_size("z") * lax.axis_size("y")
    rows_here = archive.shape[0]
    width = sketch.shape[1]
    own_rows = rows_here // (groups * CORES)
    slab_rows = len(upper_blocks(width)) * BLOCK // (groups * CORES)
    scale = math.sqrt(rows_here * stacked)
    place = jnp.stack([lax.axis_index("core"), lax.axis_index("x")]).astype(jnp.int32)

    theirs = partial_images(archive, sketch, place, groups, True)
    mine = partial_images(archive, sketch, place, groups, False)
    sums = mine + shifted(theirs, "core", 1)
    own = exchange(sums.reshape(groups, own_rows, width), "x").sum(0)

    kept, sent = gram_halves(own, place)
    gram = kept + shifted(sent, "core", 1)
    gram = exchange(gram.reshape(groups, slab_rows, BLOCK), "x").sum(0)
    across = lax.axis_size("y")
    per = pl.cdiv(slab_rows, across * 8) * 8
    split = jnp.pad(gram, ((0, per * across - slab_rows), (0, 0))).reshape(across, per, BLOCK)
    row = exchange(split, "y").sum(0)
    row = gather(row, "z").sum(0)

    near = [own, *(shifted(own, "x", s) for s in range(1, groups))]
    row, near = lax.optimization_barrier((row, near))
    far = shifted(jnp.concatenate(near, 0), "core", 1)
    far = [far[s * own_rows : (s + 1) * own_rows] for s in range(groups)]
    moved = moved_rows(archive, near, far, place, groups)

    gram = gather(row, "y").reshape(per * across, BLOCK)[:slab_rows]
    moved = exchange(moved.reshape(stacked, -1, width), over_rows)
    here = [gram, *(shifted(gram, "x", s) for s in range(1, groups))]
    there = shifted(jnp.concatenate(here, 0), "core", 1)
    there = [there[s * slab_rows : (s + 1) * slab_rows] for s in range(groups)]
    inverse, basis = factor(here + there, own, place, scale)
    return basis, last_dot(moved.sum(0), inverse, ((1,), (1,)))


def solution(mesh):
    rows, cols = mesh.devices.shape
    across = math.isqrt(rows)
    fine = Mesh(
        mesh.devices.reshape(rows // across, across, cols // CORES, CORES), ("z", "y", "x", "core")
    )
    return jax.shard_map(
        local,
        mesh=fine,
        in_specs=(P(("z", "y"), ("x", "core")), P(("x", "core"), None)),
        out_specs=(P(("z", "y", "x", "core"), None), P(("x", "core", "z", "y"), None)),
        check_vma=False,
    )
```
